512 devices in a mesh: seg: 64 (over y, x, core), tp: 8 (over z).
Axes of the slice: x: 4, y: 8, z: 8, core: 2. Of those that a mesh axis runs over, the one named last changes fastest.
Arguments:
- queries: bfloat16 [16384, 8192], P('seg', 'tp'), may hold values from -260 to 260
- key_rows: bfloat16 [16384, 1024], P('seg', 'tp'), may hold values from -4 to 4
- value_rows: bfloat16 [16384, 1024], P('seg', 'tp'), may hold values from -6 to 6
- grad_out: bfloat16 [16384, 8192], P('seg', 'tp'), may hold values from -6 to 6
- seg_order: int32 [64], replicated, may hold values from 0 to 63, each once
Outputs:
- grad_queries: bfloat16 [16384, 8192], P(('seg', 'tp'))
- grad_keys: bfloat16 [16384, 1024], P(('seg', 'tp'))
- grad_values: bfloat16 [16384, 1024], P(('seg', 'tp'))
The draws below stay inside these ranges and needn't reach their ends.
Inputs may be any that keep to these rules, and one draw needn't show every extreme that they name: `seg_order`: each position 0 to 63 once.
All inputs are finite; a program needn't handle non-finite values.
Results may differ from the reference program's by a relative error of at most 0.0065.
Values may be sent and summed in bfloat16 or wider, within the bound.
A program may use at most 64 MiB of HBM per device.

```python
import jax
import jax.numpy as jnp
from jax import lax

HEADS = 64
KV_HEADS = 8
HEAD_DIM = 128
SEG_LEN = 256
SUMM = 32
NSEG = 64
TOKENS = 16384


def shared_rows(key):
    group = HEADS // KV_HEADS
    base_k = jnp.clip(jax.random.normal(jax.random.fold_in(key, 11), (NSEG, SEG_LEN, KV_HEADS, HEAD_DIM), jnp.float32), -4.0, 4.0)
    base_q = jnp.clip(jax.random.normal(jax.random.fold_in(key, 12), (NSEG, SEG_LEN, KV_HEADS, group, HEAD_DIM), jnp.float32), -4.0, 4.0)
    return (base_q.reshape(NSEG * SEG_LEN, HEADS * HEAD_DIM), base_k.reshape(NSEG * SEG_LEN, KV_HEADS * HEAD_DIM))


def draw_queries(key, part):
    return shared_rows(key)[0].astype(jnp.bfloat16)


def draw_key_rows(key, part):
    return shared_rows(key)[1].astype(jnp.bfloat16)


def shard_levels(own_key, extent, split, low, high):
    def one(position, blocks):
        draws = jax.random.uniform(jax.random.fold_in(jax.random.fold_in(own_key, 6), position), (blocks,), jnp.float32, low / len(split), high / len(split))
        return jnp.repeat(jnp.exp(draws), extent[position] // blocks).reshape((-1,) + (1,) * (len(extent) - position - 1))

    gain = one(*split[0])
    for cut in split[1:]:
        gain = gain * one(*cut)
    return gain


def scatter_about(key, dims, scale, reach, shards=(), dtype=jnp.bfloat16):
    factor_of = shard_levels(key, dims, shards, -0.22, 0.18) if shards else 1.0
    entries = jax.random.normal(key, dims, jnp.float32) * scale * factor_of
    return jnp.minimum(jnp.maximum(entries, -reach), reach).astype(dtype)


def setup_inputs(seed: int = 0) -> dict:
    splits = jax.random.split(jax.random.key(seed), 6)
    queries = draw_queries(jax.random.fold_in(splits[5], 71), 0)
    key_rows = draw_key_rows(jax.random.fold_in(splits[5], 71), 0)
    value_rows = scatter_about(splits[2], (TOKENS, KV_HEADS * HEAD_DIM), 1.0, 6.0, ((0, 64), (1, 8)))
    grad_out = scatter_about(splits[3], (TOKENS, HEADS * HEAD_DIM), 1.0, 6.0, ((0, 64), (1, 8)))
    seg_order = jax.random.permutation(splits[4], NSEG).astype(jnp.int32)
    return {"queries": queries, "key_rows": key_rows, "value_rows": value_rows, "grad_out": grad_out, "seg_order": seg_order}


def reference(queries, key_rows, value_rows, grad_out, seg_order):
    group = HEADS // KV_HEADS
    scaling = HEAD_DIM ** -0.5
    high = lax.Precision.HIGHEST
    q_all = queries.reshape(NSEG, SEG_LEN, KV_HEADS, group, HEAD_DIM)
    g_all = grad_out.reshape(NSEG, SEG_LEN, KV_HEADS, group, HEAD_DIM)
    k_all = key_rows.reshape(NSEG, SEG_LEN, KV_HEADS, HEAD_DIM)
    v_all = value_rows.reshape(NSEG, SEG_LEN, KV_HEADS, HEAD_DIM)
    prior_k = k_all[:, SEG_LEN - SUMM:].reshape(NSEG * SUMM, KV_HEADS, HEAD_DIM)
    prior_v = v_all[:, SEG_LEN - SUMM:].reshape(NSEG * SUMM, KV_HEADS, HEAD_DIM)
    slot_order = jnp.repeat(seg_order, SUMM)
    row_pos = lax.broadcasted_iota(jnp.int32, (SEG_LEN, SEG_LEN), 0)
    col_pos = lax.broadcasted_iota(jnp.int32, (SEG_LEN, SEG_LEN), 1)
    causal = col_pos <= row_pos

    def one_segment(carry, inputs):
        q_seg, k_seg, v_seg, g_seg, order_here = inputs
        keys_f = jnp.concatenate([k_seg, prior_k], 0).astype(jnp.float32)
        vals_f = jnp.concatenate([v_seg, prior_v], 0).astype(jnp.float32)
        prior_ok = jnp.broadcast_to((slot_order < order_here)[None, :], (SEG_LEN, NSEG * SUMM))
        visible = jnp.concatenate([causal, prior_ok], 1)
        q_f = q_seg.astype(jnp.float32)
        g_f = g_seg.astype(jnp.float32)
        scores = jnp.einsum("qcgd,kcd->cgqk", q_f, keys_f, precision=high) * scaling
        scores = jnp.where(visible[None, None], scores, -jnp.inf)
        top = jnp.max(scores, -1, keepdims=True)
        weights = jnp.exp(scores - top)
        probs = weights / jnp.sum(weights, -1, keepdims=True)
        grad_probs = jnp.einsum("qcgd,kcd->cgqk", g_f, vals_f, precision=high)
        delta_rows = jnp.sum(probs * grad_probs, -1, keepdims=True)
        grad_scores = lax.optimization_barrier((probs * (grad_probs - delta_rows)).astype(jnp.bfloat16)).astype(jnp.float32)
        probs_low = lax.optimization_barrier(probs.astype(jnp.bfloat16)).astype(jnp.float32)
        grad_q = jnp.einsum("cgqk,kcd->qcgd", grad_scores, keys_f, precision=high) * scaling
        key_terms = jnp.einsum("cgqk,qcgd->kcd", grad_scores, q_f, precision=high) * scaling
        value_terms = jnp.einsum("cgqk,qcgd->kcd", probs_low, g_f, precision=high)
        new_carry = (carry[0] + key_terms[SEG_LEN:], carry[1] + value_terms[SEG_LEN:])
        return new_carry, (grad_q.astype(jnp.bfloat16), key_terms[:SEG_LEN], value_terms[:SEG_LEN])

    start = jnp.zeros((NSEG * SUMM, KV_HEADS, HEAD_DIM), jnp.float32)
    (acc_k, acc_v), (grad_q, local_k, local_v) = lax.scan(one_segment, (start, start), (q_all, k_all, v_all, g_all, seg_order))
    local_k = local_k.at[:, SEG_LEN - SUMM:].add(acc_k.reshape(NSEG, SUMM, KV_HEADS, HEAD_DIM))
    local_v = local_v.at[:, SEG_LEN - SUMM:].add(acc_v.reshape(NSEG, SUMM, KV_HEADS, HEAD_DIM))
    grad_queries = grad_q.reshape(TOKENS, HEADS * HEAD_DIM)
    grad_keys = local_k.astype(jnp.bfloat16).reshape(TOKENS, KV_HEADS * HEAD_DIM)
    grad_values = local_v.astype(jnp.bfloat16).reshape(TOKENS, KV_HEADS * HEAD_DIM)
    return grad_queries, grad_keys, grad_values
```

```python
import functools

import jax
import jax.numpy as jnp
from jax import lax
from jax.experimental import pallas as pl
from jax.experimental.pallas import tpu as pltpu
from jax.sharding import PartitionSpec as P

HEAD_DIM = 128
SUMM = 32
SEG = 256
NY, NX, NZ = 8, 4, 8
GROUP = 8
CHUNKS = 9
SCALE = HEAD_DIM**-0.5
SCALE_LOG2 = SCALE * 1.4426950408889634
HIDDEN = -1e30
BF = jnp.bfloat16
F32 = jnp.float32
MESH = pl.DeviceIdType.MESH


def dot(a, b):
    return jnp.dot(a, b, preferred_element_type=F32)


def dot_t(a, b):
    return lax.dot_general(a, b, (((1,), (1,)), ((), ())), preferred_element_type=F32)


def kernel(
    order_ref, q_ref, k_ref, v_ref, g_ref, oq_ref, ok_ref, ov_ref,
    bias, buf, s_ref, dp_ref, e_ref, ds_ref, qp_ref, gp_ref, kt_ref, dq_ref,
    sib_out, sib_in, x_out, x_in, x_own, y_out, y_in, local, summ, final,
    gy_s, gy_r, gx_s, gx_r, gs_s, gs_r, rs_s, rs_r, rx_s, rx_r, ry_s, ry_r, q_s, q_r, k_s, k_r, v_s, v_r,
):
    seg = lax.axis_index("seg")
    z = lax.axis_index("tp")
    core = lax.rem(seg, 2)
    x = lax.rem(seg // 2, NX)
    y = seg // (2 * NX)
    mine = x * 2 + core

    def seg_dev(yy, xx, cc):
        return {"seg": (yy * NX + xx) * 2 + cc}

    def y_dev(r):
        return seg_dev(lax.rem(y + r, NY), x, core)

    def x_dev(r):
        return seg_dev(y, lax.rem(x + r, NX), core)

    def z_dev(r):
        return {"tp": lax.rem(z + r, NZ)}

    sibling = seg_dev(y, x, 1 - core)

    def remote(src, dst, send, recv, dev):
        return pltpu.make_async_remote_copy(
            src_ref=src, dst_ref=dst, send_sem=send, recv_sem=recv, device_id=dev, device_id_type=MESH
        )

    barrier = pltpu.get_barrier_semaphore()
    peers = [y_dev(r) for r in range(1, NY)] + [x_dev(r) for r in range(1, NX)]
    peers += [sibling] + [z_dev(r) for r in range(1, NZ)]
    for dev in peers:
        pl.semaphore_signal(barrier, inc=1, device_id=dev, device_id_type=MESH)
    pl.semaphore_wait(barrier, len(peers))

    buf[mine, y, 0] = k_ref[SEG - SUMM :, :]
    buf[mine, y, 1] = v_ref[SEG - SUMM :, :]
    gy = {}
    for r in (4, 3, 5, 2, 6, 1, 7):
        gy[r] = remote(buf.at[mine, y], buf.at[mine, y], gy_s.at[r], gy_r.at[r], y_dev(r))
        gy[r].start()
    own = order_ref[seg]
    for xc in range(2 * NX):
        for yy in range(NY):
            bias[xc * NY + yy] = jnp.where(order_ref[yy * 2 * NX + xc] < own, 0.0, HIDDEN)
    kt_ref[:, :SEG] = k_ref[...].T
    for r in range(1, NY):
        gy[r].wait_recv()
    gx = {}
    for r in (2, 1, 3):
        gx[r] = remote(buf.at[mine], buf.at[mine], gx_s.at[r], gx_r.at[r], x_dev(r))
        gx[r].start()
    gs = {0: remote(buf.at[mine], buf.at[mine], gs_s.at[0], gs_r.at[0], sibling)}
    gs[0].start()
    for r in (1, 3, 2):
        gx[r].wait_recv()
        block = lax.rem(x + NX - r, NX) * 2 + core
        gs[r] = remote(buf.at[block], buf.at[block], gs_s.at[r], gs_r.at[r], sibling)
        gs[r].start()
    for r in range(NX):
        gs[r].wait_recv()
    for r in range(1, NY):
        gy[r].wait_send()
    for r in range(1, NX):
        gx[r].wait_send()
    for r in range(NX):
        gs[r].wait_send()

    def keys(c):
        return k_ref[...] if c == 0 else buf[c - 1, :, 0].reshape(SEG, HEAD_DIM)

    def values(c):
        return v_ref[...] if c == 0 else buf[c - 1, :, 1].reshape(SEG, HEAD_DIM)

    for c in range(1, CHUNKS):
        kt_ref[:, c * SEG : (c + 1) * SEG] = keys(c).T

    def fold(a, op):
        return op(a.reshape(SEG // 8, 8, SEG), 0)

    def dq_copy(h, r):
        to = lax.rem(z + r, NZ)
        return remote(
            dq_ref.at[h, pl.ds(to * SUMM, SUMM), :],
            oq_ref.at[:, pl.ds(pl.multiple_of((z * GROUP + h) * HEAD_DIM, HEAD_DIM), HEAD_DIM)],
            q_s.at[r], q_r.at[r], z_dev(r),
        )

    def head(h, carry):
        cols = pl.ds(pl.multiple_of(h * HEAD_DIM, HEAD_DIM), HEAD_DIM)
        wide = pl.ds(pl.multiple_of(h * SEG, SEG), SEG)
        qh = q_ref[:, cols]
        gh = g_ref[:, cols]
        top = jnp.full((8, SEG), HIDDEN, F32)
        for c in range(CHUNKS):
            rows = slice(c * SEG, (c + 1) * SEG)
            s = dot_t(keys(c), qh)
            if c == 0:
                key_pos = lax.broadcasted_iota(jnp.int32, (SEG, SEG), 0)
                query_pos = lax.broadcasted_iota(jnp.int32, (SEG, SEG), 1)
                s = jnp.where(key_pos <= query_pos, s, HIDDEN)
            else:
                s = jnp.concatenate(
                    [s[SUMM * t : SUMM * (t + 1)] + bias[(c - 1) * NY + t] for t in range(NY)], 0
                )
            s_ref[rows, :] = s
            top = jnp.maximum(top, fold(s, jnp.max))
        top = jnp.max(top, 0, keepdims=True) * SCALE_LOG2
        total = jnp.zeros((8, SEG), F32)
        delta = jnp.zeros((8, SEG), F32)
        for c in range(CHUNKS):
            rows = slice(c * SEG, (c + 1) * SEG)
            e = jnp.exp2(s_ref[rows, :] * SCALE_LOG2 - top)
            dp = dot_t(values(c), gh)
            total = total + fold(e, jnp.sum)
            delta = delta + fold(e * dp, jnp.sum)
            e_ref[rows, wide] = e.astype(BF)
            dp_ref[rows, :] = dp
        inv = 1.0 / jnp.sum(total, 0, keepdims=True)
        delta = jnp.sum(delta, 0, keepdims=True) * inv
        acc = jnp.zeros((HEAD_DIM, SEG), F32)
        for c in range(CHUNKS):
            rows = slice(c * SEG, (c + 1) * SEG)
            ds = (e_ref[rows, wide].astype(F32) * (dp_ref[rows, :] - delta)).astype(BF)
            ds_ref[rows, wide] = ds
            acc = acc + dot(kt_ref[:, rows], ds)
        dq_ref[h] = (acc * (inv * SCALE)).T.astype(BF)
        for r in (4, 3, 5, 2, 6, 1, 7):
            dq_copy(h, r).start()
        inv_rows = jnp.broadcast_to(inv, (HEAD_DIM, SEG)).T
        qp_ref[wide, :] = (qh.astype(F32) * (inv_rows * SCALE)).astype(BF)
        gp_ref[wide, :] = (gh.astype(F32) * inv_rows).astype(BF)
        return carry

    lax.fori_loop(0, GROUP, head, 0)

    def terms(c):
        rows = pl.ds(pl.multiple_of(c * SEG, SEG), SEG)
        return dot(ds_ref[rows, :], qp_ref[...]), dot(e_ref[rows, :], gp_ref[...])

    def split(a):
        return a.reshape(NY, SUMM, HEAD_DIM)

    rs, rx, ry = {}, {}, {}
    for r in (2, 1, 3, 0):
        xx = lax.rem(x + r, NX)
        dk, dv = terms(1 + xx * 2 + 1 - core)
        sib_out[r, :, 0] = split(dk).astype(BF)
        sib_out[r, :, 1] = split(dv).astype(BF)
        rs[r] = remote(sib_out.at[r], sib_in.at[r], rs_s.at[r], rs_r.at[r], sibling)
        rs[r].start()
        dk, dv = terms(1 + xx * 2 + core)
        rs[r].wait_recv()
        dk = split(dk) + sib_in[r, :, 0].astype(F32)
        dv = split(dv) + sib_in[r, :, 1].astype(F32)
        if r:
            x_out[r, :, 0] = dk.astype(BF)
            x_out[r, :, 1] = dv.astype(BF)
            rx[r] = remote(x_out.at[r], x_in.at[r], rx_s.at[r], rx_r.at[r], x_dev(r))
            rx[r].start()
        else:
            x_own[:, 0] = dk
            x_own[:, 1] = dv
    dk, dv = terms(0)
    local[0] = dk.astype(BF)
    local[1] = dv.astype(BF)
    summ[0] = dk[SEG - SUMM :]
    summ[1] = dv[SEG - SUMM :]

    my_cols = pl.ds(pl.multiple_of(z * HEAD_DIM, HEAD_DIM), HEAD_DIM)

    def kv_copies(r, src_k, src_v):
        return (
            remote(src_k, ok_ref.at[:, my_cols], k_s.at[r], k_r.at[r], z_dev(r)),
            remote(src_v, ov_ref.at[:, my_cols], v_s.at[r], v_r.at[r], z_dev(r)),
        )

    def early(r):
        rows = pl.ds(lax.rem(z + r, NZ) * SUMM, SUMM)
        return kv_copies(r, local.at[0, rows, :], local.at[1, rows, :])

    for r in range(1, NZ):

        @pl.when(lax.rem(z + r, NZ) != NZ - 1)
        def _(r=r):
            for copy in early(r):
                copy.start()

    for r in (1, 3, 2):
        rx[r].wait_recv()
    acc = x_own[...]
    for r in range(1, NX):
        acc = acc + x_in[r].astype(F32)
    x_own[...] = acc
    y_out[...] = acc.astype(BF)
    for r in (4, 3, 5, 2, 6, 1, 7):
        ry[r] = remote(y_out.at[lax.rem(y + r, NY)], y_in.at[r], ry_s.at[r], ry_r.at[r], y_dev(r))
        ry[r].start()
    acc = x_own[y] + summ[...]
    for r in range(1, NY):
        ry[r].wait_recv()
        acc = acc + y_in[r].astype(F32)
    final[...] = acc.astype(BF)
    for r in range(1, NZ):

        @pl.when(lax.rem(z + r, NZ) == NZ - 1)
        def _(r=r):
            for copy in kv_copies(r, final.at[0], final.at[1]):
                copy.start()

    my_rows = pl.ds(z * SUMM, SUMM)
    oq_cols = pl.ds(pl.multiple_of(z * GROUP * HEAD_DIM, GROUP * HEAD_DIM), GROUP * HEAD_DIM)
    oq_ref[:, oq_cols] = jnp.concatenate([dq_ref[h, my_rows, :] for h in range(GROUP)], 1)

    @pl.when(z != NZ - 1)
    def _():
        ok_ref[:, my_cols] = local[0, my_rows, :]
        ov_ref[:, my_cols] = local[1, my_rows, :]

    @pl.when(z == NZ - 1)
    def _():
        ok_ref[:, my_cols] = final[0]
        ov_ref[:, my_cols] = final[1]

    for r in range(1, NZ):
        for copy in early(r):
            copy.wait()
        whole = remote(oq_ref.at[:, oq_cols], oq_ref.at[:, oq_cols], q_s.at[r], q_r.at[r], z_dev(r))
        whole.wait()
    for r in range(NX):
        rs[r].wait_send()
    for r in range(1, NX):
        rx[r].wait_send()
    for r in range(1, NY):
        ry[r].wait_send()


def local(queries, key_rows, value_rows, grad_out, seg_order):
    vmem = pl.BlockSpec(memory_space=pltpu.VMEM)
    smem = pl.BlockSpec(memory_space=pltpu.SMEM)
    width = CHUNKS * SEG
    block = (NY, 2, SUMM, HEAD_DIM)
    sems = [NY, NY, NX, NX, NX, NX, NX, NX, NX, NX, NY, NY, NZ, NZ, NZ, NZ, NZ, NZ]
    return pl.pallas_call(
        kernel,
        out_shape=[
            jax.ShapeDtypeStruct((SUMM, NZ * GROUP * HEAD_DIM), BF),
            jax.ShapeDtypeStruct((SUMM, NZ * HEAD_DIM), BF),
            jax.ShapeDtypeStruct((SUMM, NZ * HEAD_DIM), BF),
        ],
        in_specs=[smem, vmem, vmem, vmem, vmem],
        out_specs=[vmem, vmem, vmem],
        scratch_shapes=[
            pltpu.SMEM((2 * NX * NY,), F32),
            pltpu.VMEM((2 * NX,) + block, BF),
            pltpu.VMEM((width, SEG), F32),
            pltpu.VMEM((width, SEG), F32),
            pltpu.VMEM((width, GROUP * SEG), BF),
            pltpu.VMEM((width, GROUP * SEG), BF),
            pltpu.VMEM((GROUP * SEG, HEAD_DIM), BF),
            pltpu.VMEM((GROUP * SEG, HEAD_DIM), BF),
            pltpu.VMEM((HEAD_DIM, width), BF),
            pltpu.VMEM((GROUP, SEG, HEAD_DIM), BF),
            pltpu.VMEM((NX,) + block, BF),
            pltpu.VMEM((NX,) + block, BF),
            pltpu.VMEM((NX,) + block, BF),
            pltpu.VMEM((NX,) + block, BF),
            pltpu.VMEM(block, F32),
            pltpu.VMEM(block, BF),
            pltpu.VMEM(block, BF),
            pltpu.VMEM((2, SEG, HEAD_DIM), BF),
            pltpu.VMEM((2, SUMM, HEAD_DIM), F32),
            pltpu.VMEM((2, SUMM, HEAD_DIM), BF),
        ]
        + [pltpu.SemaphoreType.DMA((n,)) for n in sems],
        compiler_params=pltpu.CompilerParams(
            collective_id=0, has_side_effects=True, vmem_limit_bytes=56 * 2**20
        ),
        name="attention_backward",
    )(seg_order, queries, key_rows, value_rows, grad_out)


def solution(mesh):
    in_specs = (P("seg", "tp"), P("seg", "tp"), P("seg", "tp"), P("seg", "tp"), P())
    out_specs = (P(("seg", "tp"), None), P(("seg", "tp"), None), P(("seg", "tp"), None))
    return jax.shard_map(local, mesh=mesh, in_specs=in_specs, out_specs=out_specs, check_vma=False)
```

```python
import jax
import jax.numpy as jnp
from jax import lax
from jax.experimental import pallas as pl
from jax.experimental.pallas import tpu as pltpu
from jax.sharding import PartitionSpec as P

HEAD_DIM = 128
SUMM = 32
SEG = 256
NY, NX, NZ = 8, 4, 8
GROUP = 8
CHUNKS = 9
SCALE = HEAD_DIM**-0.5
SCALE_LOG2 = SCALE * 1.4426950408889634
HIDDEN = -1e30
BF = jnp.bfloat16
F32 = jnp.float32
MESH = pl.DeviceIdType.MESH
KEYS, VALUES = 0, 1
FAR_FIRST = (4, 3, 5, 2, 6, 1, 7)


def dot(a, b):
    return jnp.dot(a, b, preferred_element_type=F32)


def dot_t(a, b):
    return lax.dot_general(a, b, (((1,), (1,)), ((), ())), preferred_element_type=F32)


def split(a):
    return a.reshape(NY, SUMM, HEAD_DIM)


def fold(a, op):
    return op(a.reshape(SEG // 8, 8, SEG), 0)


def rows_of(slot):
    return slice(slot * SEG, (slot + 1) * SEG)


def aligned(index, size):
    return pl.ds(pl.multiple_of(index * size, size), size)


def kernel(
    order_ref, q_hbm, k_hbm, v_hbm, g_hbm, oq_ref, ok_ref, ov_ref,
    bias, q_ref, k_ref, v_ref, g_ref, buf, s_ref, dp_ref, e_ref, qp_ref, gp_ref, kt_ref, dq_ref,
    top_ref, inv_ref, delta_ref,
    sib_out, sib_in, parts, x_out, x_in, x_own, y_out, y_in, local, summ, final,
    in_sem, own_sem, gy_s, gy_r, gx_s, gx_r, gs_s, gs_r,
    rs_s, rs_r, rx_s, rx_r, ry_s, ry_r, q_s, q_r, z_s, z_r,
):
    seg = lax.axis_index("seg")
    z = lax.axis_index("tp")
    core = lax.rem(seg, 2)
    x = lax.rem(seg // 2, NX)
    y = seg // (2 * NX)

    def seg_dev(yy, xx, cc):
        return {"seg": (yy * NX + xx) * 2 + cc}

    def y_dev(r):
        return seg_dev(lax.rem(y + r, NY), x, core)

    def x_dev(r):
        return seg_dev(y, lax.rem(x + r, NX), core)

    def z_dev(r):
        return {"tp": lax.rem(z + r, NZ)}

    sibling = seg_dev(y, x, 1 - core)

    def column(d, cc):
        return lax.rem(x + d, NX) * 2 + cc

    def remote(src, dst, send, recv, dev):
        return pltpu.make_async_remote_copy(
            src_ref=src, dst_ref=dst, send_sem=send, recv_sem=recv, device_id=dev, device_id_type=MESH
        )

    mine = column(0, core)
    fetch = [
        pltpu.make_async_copy(k_hbm.at[pl.ds(SEG - SUMM, SUMM), :], buf.at[KEYS, mine, y], in_sem.at[0]),
        pltpu.make_async_copy(v_hbm.at[pl.ds(SEG - SUMM, SUMM), :], buf.at[VALUES, mine, y], in_sem.at[1]),
        pltpu.make_async_copy(k_hbm, k_ref, in_sem.at[2]),
        pltpu.make_async_copy(q_hbm, q_ref, in_sem.at[3]),
        pltpu.make_async_copy(v_hbm, v_ref, in_sem.at[4]),
        pltpu.make_async_copy(g_hbm, g_ref, in_sem.at[5]),
    ]
    for copy in fetch:
        copy.start()
    barrier = pltpu.get_barrier_semaphore()
    peers = [y_dev(r) for r in range(1, NY)] + [x_dev(r) for r in range(1, NX)]
    peers += [sibling] + [z_dev(r) for r in range(1, NZ)]
    for dev in peers:
        pl.semaphore_signal(barrier, inc=1, device_id=dev, device_id_type=MESH)
    sends = []

    def go(copy):
        copy.start()
        sends.append(copy)
        return copy

    fetch[0].wait()
    fetch[1].wait()
    pl.semaphore_wait(barrier, len(peers))

    gy, gs = {}, {}
    for t in (KEYS, VALUES):
        for r in FAR_FIRST:
            gy[t, r] = go(
                remote(buf.at[t, mine, y], buf.at[t, mine, y], gy_s.at[t, r], gy_r.at[t, r], y_dev(r))
            )

    def spread_x(t, block):
        for r in (2, 1, 3):
            remote(block, block, gx_s.at[t, r], gx_r.at[t, r], x_dev(r)).start()

    def column_x(t, r):
        block = buf.at[t, mine]
        return remote(block, block, gx_s.at[t, r], gx_r.at[t, r], x_dev(r))

    def to_sibling(t, d):
        block = buf.at[t, column(d, core)]
        gs[t, d] = go(remote(block, block, gs_s.at[t, d], gs_r.at[t, d], sibling))

    def gather_y(t):
        spread_x(t, buf.at[t, mine, y])
        for r in (1, 7, 2, 6, 3, 5, 4):
            gy[t, r].wait_recv()
            spread_x(t, buf.at[t, mine, lax.rem(y + NY - r, NY)])
        to_sibling(t, 0)
        for r in range(1, NX):
            sends.append(column_x(t, r))

    def gather_x(t, d):
        column_x(t, NX - d).wait_recv()
        to_sibling(t, d)

    def block_of(slot):
        return column((slot - 1) // 2, core if slot % 2 else 1 - core)

    def fetched(t, slot):
        if slot == 0:
            return (k_ref if t == KEYS else v_ref)[...]
        return buf[t, block_of(slot)].reshape(SEG, HEAD_DIM)

    def scores(slot):
        kc = fetched(KEYS, slot)
        rows = rows_of(slot)
        kt_ref[:, rows] = kc.T
        for h in range(GROUP):
            s = dot_t(kc, q_ref[:, h * HEAD_DIM : (h + 1) * HEAD_DIM]) * SCALE_LOG2
            if slot:
                s = jnp.concatenate(
                    [s[SUMM * i : SUMM * (i + 1)] + bias[block_of(slot) * NY + i] for i in range(NY)], 0
                )
            else:
                key_pos = lax.broadcasted_iota(jnp.int32, (SEG, SEG), 0)
                query_pos = lax.broadcasted_iota(jnp.int32, (SEG, SEG), 1)
                s = jnp.where(key_pos <= query_pos, s, HIDDEN)
            s_ref[h, rows, :] = s
            top = fold(s, jnp.max)
            top_ref[h] = jnp.maximum(top_ref[h], top) if slot else top

    def mask_terms():
        own = order_ref[seg]
        for xc in range(2 * NX):
            for yy in range(NY):
                bias[xc * NY + yy] = jnp.where(order_ref[yy * 2 * NX + xc] < own, 0.0, HIDDEN)

    mask_terms()
    for copy in fetch[2:]:
        copy.wait()
    scores(0)
    gather_y(KEYS)
    scores(1)
    gs[KEYS, 0].wait_recv()
    scores(2)
    gather_y(VALUES)
    for d in (3, 1, 2):
        gather_x(KEYS, d)
    scores(7)
    scores(3)
    scores(5)
    for d in (3, 1, 2):
        gs[KEYS, d].wait_recv()
    scores(8)
    scores(4)
    scores(6)

    def weigh(h):
        cols = aligned(h, HEAD_DIM)
        wide = aligned(h, SEG)
        top = jnp.max(top_ref[h], 0, keepdims=True)
        total = jnp.zeros((8, SEG), F32)
        for slot in range(CHUNKS):
            rows = rows_of(slot)
            e = jnp.exp2(s_ref[h, rows, :] - top)
            total = total + fold(e, jnp.sum)
            e_ref[rows, wide] = e.astype(BF)
        inv = 1.0 / jnp.sum(total, 0, keepdims=True)
        inv_ref[h] = inv
        inv_rows = jnp.broadcast_to(inv, (HEAD_DIM, SEG)).T
        qp_ref[wide, :] = (q_ref[:, cols].astype(F32) * (inv_rows * SCALE)).astype(BF)
        gp_ref[wide, :] = (g_ref[:, cols].astype(F32) * inv_rows).astype(BF)

    def weigh_pair(i, carry):
        weigh(2 * i)
        weigh(2 * i + 1)
        return carry

    lax.fori_loop(0, GROUP // 2, weigh_pair, 0)

    def weigh_products(h):
        cols = aligned(h, HEAD_DIM)
        wide = aligned(h, SEG)
        gh = g_ref[:, cols]
        delta = jnp.zeros((8, SEG), F32)
        for slot in range(CHUNKS):
            rows = rows_of(slot)
            dp = dot_t(fetched(VALUES, slot), gh)
            delta = delta + fold(e_ref[rows, wide].astype(F32) * dp, jnp.sum)
            dp_ref[h, rows, :] = dp
        delta_ref[h] = jnp.sum(delta, 0, keepdims=True) * inv_ref[h]

    def products_pair(i, carry):
        weigh_products(2 * i)
        weigh_products(2 * i + 1)
        return carry

    my_cols = aligned(z, HEAD_DIM)
    my_rows = pl.ds(z * SUMM, SUMM)
    outs = (ok_ref, ov_ref)

    def terms(t, slot):
        return dot(e_ref[rows_of(slot), :], (qp_ref if t == KEYS else gp_ref)[...])

    rs, rx, ry = {}, {}, {}

    def z_copy(t, r, src):
        return remote(src, outs[t].at[:, my_cols], z_s.at[t, r], z_r.at[t, r], z_dev(r))

    def early(t, r):
        return z_copy(t, r, local.at[t, pl.ds(lax.rem(z + r, NZ) * SUMM, SUMM), :])

    def score_grads(slot):
        rows = rows_of(slot)
        for h in range(GROUP):
            wide = slice(h * SEG, (h + 1) * SEG)
            e_ref[rows, wide] = (
                e_ref[rows, wide].astype(F32) * (dp_ref[h, rows, :] - delta_ref[h])
            ).astype(BF)

    def reduce_x(t):
        for d in (2, 1, 3, 0):
            sib_out[t, d] = split(terms(t, 2 + 2 * d)).astype(BF)
        for d in (2, 1, 3, 0):
            rs[t, d] = go(remote(sib_out.at[t, d], sib_in.at[t, d], rs_s.at[t, d], rs_r.at[t, d], sibling))
        for d in (2, 1, 3, 0):
            parts[d] = split(terms(t, 1 + 2 * d))
        for d in (2, 1, 3, 0):
            rs[t, d].wait_recv()
            part = parts[d] + sib_in[t, d].astype(F32)
            if d:
                x_out[t, d] = part.astype(BF)
                rx[t, d] = go(remote(x_out.at[t, d], x_in.at[t, d], rx_s.at[t, d], rx_r.at[t, d], x_dev(d)))
            else:
                x_own[t] = part
        part = terms(t, 0)
        local[t] = part.astype(BF)
        summ[t] = part[SEG - SUMM :]
        for r in range(1, NZ):

            @pl.when(lax.rem(z + r, NZ) != NZ - 1)
            def _(r=r):
                early(t, r).start()

    def reduce_y(t):
        acc = x_own[t]
        for d in (1, 3, 2):
            rx[t, d].wait_recv()
            acc = acc + x_in[t, d].astype(F32)
        x_own[t] = acc
        y_out[t] = acc.astype(BF)
        for r in FAR_FIRST:
            ry[t, r] = go(
                remote(y_out.at[t, lax.rem(y + r, NY)], y_in.at[t, r], ry_s.at[t, r], ry_r.at[t, r], y_dev(r))
            )

    def reduce_end(t):
        acc = x_own[t, y] + summ[t]
        for r in range(1, NY):
            ry[t, r].wait_recv()
            acc = acc + y_in[t, r].astype(F32)
        final[t] = acc.astype(BF)
        for r in range(1, NZ):

            @pl.when(lax.rem(z + r, NZ) == NZ - 1)
            def _(r=r):
                z_copy(t, r, final.at[t]).start()

        @pl.when(z != NZ - 1)
        def _():
            pltpu.make_async_copy(local.at[t, my_rows, :], outs[t].at[:, my_cols], own_sem.at[t]).start()

        @pl.when(z == NZ - 1)
        def _():
            pltpu.make_async_copy(final.at[t], outs[t].at[:, my_cols], own_sem.at[t]).start()

    def dq_cols(h):
        return aligned(z * GROUP + h, HEAD_DIM)

    def query_grads(first):
        for h in (first, first + 1):
            acc = dot(kt_ref[...], e_ref[:, h * SEG : (h + 1) * SEG])
            dq_ref[h] = (acc * (inv_ref[h] * SCALE)).T.astype(BF)
        for h in (first, first + 1):
            for r in FAR_FIRST:
                to = pl.ds(lax.rem(z + r, NZ) * SUMM, SUMM)
                remote(dq_ref.at[h, to, :], oq_ref.at[:, dq_cols(h)], q_s.at[r], q_r.at[r], z_dev(r)).start()

    for d in (3, 1, 2):
        gather_x(VALUES, d)
    reduce_x(VALUES)
    for d in range(NX):
        gs[VALUES, d].wait_recv()
    lax.fori_loop(0, GROUP // 2, products_pair, 0)
    for slot in range(CHUNKS):
        score_grads(slot)
    query_grads(0)
    reduce_y(VALUES)
    reduce_x(KEYS)
    query_grads(2)
    query_grads(4)
    query_grads(6)
    own_dq = [
        pltpu.make_async_copy(dq_ref.at[h, my_rows, :], oq_ref.at[:, dq_cols(h)], in_sem.at[h])
        for h in range(GROUP)
    ]
    for copy in own_dq:
        copy.start()
    reduce_end(VALUES)
    reduce_y(KEYS)
    reduce_end(KEYS)

    for copy in own_dq:
        copy.wait()
    oq_cols = aligned(z, GROUP * HEAD_DIM)
    for r in range(1, NZ):
        remote(oq_ref.at[:, oq_cols], oq_ref.at[:, oq_cols], q_s.at[r], q_r.at[r], z_dev(r)).wait()
    for t in (VALUES, KEYS):
        for r in range(1, NZ):
            early(t, r).wait()
        pltpu.make_async_copy(final.at[t], outs[t].at[:, my_cols], own_sem.at[t]).wait()
    for copy in sends:
        copy.wait_send()


def place(a_ref, b_ref, c_ref, oa_ref, ob_ref, oc_ref, sem):
    copies = [
        pltpu.make_async_copy(src, dst, sem.at[i])
        for i, (src, dst) in enumerate(((a_ref, oa_ref), (b_ref, ob_ref), (c_ref, oc_ref)))
    ]
    for copy in copies:
        copy.start()
    for copy in copies:
        copy.wait()


def backward(queries, key_rows, value_rows, grad_out, seg_order):
    hbm = pl.BlockSpec(memory_space=pl.ANY)
    smem = pl.BlockSpec(memory_space=pltpu.SMEM)
    width = CHUNKS * SEG
    column = (NY, SUMM, HEAD_DIM)
    outs = [
        jax.ShapeDtypeStruct((SUMM, NZ * GROUP * HEAD_DIM), BF),
        jax.ShapeDtypeStruct((SUMM, NZ * HEAD_DIM), BF),
        jax.ShapeDtypeStruct((SUMM, NZ * HEAD_DIM), BF),
    ]
    scratch = [
        pltpu.SMEM((2 * NX * NY,), F32),
        pltpu.VMEM((SEG, GROUP * HEAD_DIM), BF),
        pltpu.VMEM((SEG, HEAD_DIM), BF),
        pltpu.VMEM((SEG, HEAD_DIM), BF),
        pltpu.VMEM((SEG, GROUP * HEAD_DIM), BF),
        pltpu.VMEM((2, 2 * NX) + column, BF),
        pltpu.VMEM((GROUP, width, SEG), F32),
        pltpu.VMEM((GROUP, width, SEG), F32),
        pltpu.VMEM((width, GROUP * SEG), BF),
        pltpu.VMEM((GROUP * SEG, HEAD_DIM), BF),
        pltpu.VMEM((GROUP * SEG, HEAD_DIM), BF),
        pltpu.VMEM((HEAD_DIM, width), BF),
        pltpu.VMEM((GROUP, SEG, HEAD_DIM), BF),
        pltpu.VMEM((GROUP, 8, SEG), F32),
        pltpu.VMEM((GROUP, 1, SEG), F32),
        pltpu.VMEM((GROUP, 1, SEG), F32),
        pltpu.VMEM((2, NX) + column, BF),
        pltpu.VMEM((2, NX) + column, BF),
        pltpu.VMEM((NX,) + column, F32),
        pltpu.VMEM((2, NX) + column, BF),
        pltpu.VMEM((2, NX) + column, BF),
        pltpu.VMEM((2,) + column, F32),
        pltpu.VMEM((2,) + column, BF),
        pltpu.VMEM((2,) + column, BF),
        pltpu.VMEM((2, SEG, HEAD_DIM), BF),
        pltpu.VMEM((2, SUMM, HEAD_DIM), F32),
        pltpu.VMEM((2, SUMM, HEAD_DIM), BF),
    ]
    pairs = [(2, NY), (2, NX), (2, NX), (2, NX), (2, NX), (2, NY), (NZ,), (2, NZ)]
    scratch += [pltpu.SemaphoreType.DMA((8,)), pltpu.SemaphoreType.DMA((2,))]
    scratch += [pltpu.SemaphoreType.DMA(shape) for shape in pairs for _ in range(2)]
    raw = pl.pallas_call(
        kernel,
        out_shape=outs,
        in_specs=[smem, hbm, hbm, hbm, hbm],
        out_specs=[hbm, hbm, hbm],
        scratch_shapes=scratch,
        compiler_params=pltpu.CompilerParams(
            collective_id=0, has_side_effects=True, vmem_limit_bytes=60 * 2**20
        ),
        name="attention_backward",
    )(seg_order, queries, key_rows, value_rows, grad_out)
    return pl.pallas_call(
        place,
        out_shape=outs,
        in_specs=[pl.BlockSpec(memory_space=pltpu.VMEM)] * 3,
        out_specs=[hbm, hbm, hbm],
        scratch_shapes=[pltpu.SemaphoreType.DMA((3,))],
        name="place",
    )(*raw)


def solution(mesh):
    in_specs = (P("seg", "tp"), P("seg", "tp"), P("seg", "tp"), P("seg", "tp"), P())
    out_specs = (P(("seg", "tp"), None), P(("seg", "tp"), None), P(("seg", "tp"), None))
    return jax.shard_map(backward, mesh=mesh, in_specs=in_specs, out_specs=out_specs, check_vma=False)
```

```python
import jax
import jax.numpy as jnp
from jax import lax
from jax.experimental import pallas as pl
from jax.experimental.pallas import tpu as pltpu
from jax.sharding import PartitionSpec as P

HEAD_DIM = 128
SUMM = 32
SEG = 256
NY, NX, NZ = 8, 4, 8
GROUP = 8
CHUNKS = 9
SCALE = HEAD_DIM**-0.5
SCALE_LOG2 = SCALE * 1.4426950408889634
HIDDEN = -1e30
BF = jnp.bfloat16
F32 = jnp.float32
MESH = pl.DeviceIdType.MESH
KEYS, VALUES = 0, 1
FAR_FIRST = (4, 3, 5, 2, 6, 1, 7)


def dot(a, b):
    return jnp.dot(a, b, preferred_element_type=F32)


def dot_t(a, b):
    return lax.dot_general(a, b, (((1,), (1,)), ((), ())), preferred_element_type=F32)


def split(a):
    return a.reshape(NY, SUMM, HEAD_DIM)


def fold(a, op):
    return op(a.reshape(SEG // 8, 8, SEG), 0)


def rows_of(slot):
    return slice(slot * SEG, (slot + 1) * SEG)


def aligned(index, size):
    return pl.ds(pl.multiple_of(index * size, size), size)


def kernel(
    order_ref, q_hbm, k_hbm, v_hbm, g_hbm, oq_ref, ok_ref, ov_ref,
    bias, q_ref, k_ref, v_ref, g_ref, buf, s_ref, dp_ref, e_ref, ds_ref, qs_ref, gs_ref, kt_ref, dq_ref,
    top_ref, total_ref, delta_ref,
    sib_out, sib_in, parts, x_out, x_in, x_own, y_out, y_in, local, summ, final,
    in_sem, own_sem, gy_s, gy_r, gx_s, gx_r, gs_s, gs_r,
    rs_s, rs_r, rx_s, rx_r, ry_s, ry_r, q_s, q_r, z_s, z_r,
):
    seg = lax.axis_index("seg")
    z = lax.axis_index("tp")
    core = lax.rem(seg, 2)
    x = lax.rem(seg // 2, NX)
    y = seg // (2 * NX)

    def seg_dev(yy, xx, cc):
        return {"seg": (yy * NX + xx) * 2 + cc}

    def y_dev(r):
        return seg_dev(lax.rem(y + r, NY), x, core)

    def x_dev(r):
        return seg_dev(y, lax.rem(x + r, NX), core)

    def z_dev(r):
        return {"tp": lax.rem(z + r, NZ)}

    sibling = seg_dev(y, x, 1 - core)

    def column(d, cc):
        return lax.rem(x + d, NX) * 2 + cc

    def remote(src, dst, send, recv, dev):
        return pltpu.make_async_remote_copy(
            src_ref=src, dst_ref=dst, send_sem=send, recv_sem=recv, device_id=dev, device_id_type=MESH
        )

    mine = column(0, core)
    fetch = [
        pltpu.make_async_copy(k_hbm.at[pl.ds(SEG - SUMM, SUMM), :], buf.at[KEYS, mine, y], in_sem.at[0]),
        pltpu.make_async_copy(v_hbm.at[pl.ds(SEG - SUMM, SUMM), :], buf.at[VALUES, mine, y], in_sem.at[1]),
        pltpu.make_async_copy(k_hbm, k_ref, in_sem.at[2]),
        pltpu.make_async_copy(q_hbm, q_ref, in_sem.at[3]),
        pltpu.make_async_copy(v_hbm, v_ref, in_sem.at[4]),
        pltpu.make_async_copy(g_hbm, g_ref, in_sem.at[5]),
    ]
    for copy in fetch:
        copy.start()
    barrier = pltpu.get_barrier_semaphore()
    peers = [y_dev(r) for r in FAR_FIRST] + [x_dev(r) for r in range(1, NX)]
    peers += [sibling] + [z_dev(r) for r in range(1, NZ)]
    for dev in peers:
        pl.semaphore_signal(barrier, inc=1, device_id=dev, device_id_type=MESH)
    sends = []

    def go(copy):
        copy.start()
        sends.append(copy)
        return copy

    fetch[0].wait()
    fetch[1].wait()
    pl.semaphore_wait(barrier, len(peers))

    gy, gs = {}, {}
    for t in (KEYS, VALUES):
        for r in FAR_FIRST:
            gy[t, r] = go(
                remote(buf.at[t, mine, y], buf.at[t, mine, y], gy_s.at[t, r], gy_r.at[t, r], y_dev(r))
            )

    def spread_x(t, block):
        for r in (2, 1, 3):
            remote(block, block, gx_s.at[t, r], gx_r.at[t, r], x_dev(r)).start()

    def column_x(t, r):
        block = buf.at[t, mine]
        return remote(block, block, gx_s.at[t, r], gx_r.at[t, r], x_dev(r))

    def to_sibling(t, d):
        block = buf.at[t, column(d, core)]
        gs[t, d] = go(remote(block, block, gs_s.at[t, d], gs_r.at[t, d], sibling))

    def gather_y(t):
        spread_x(t, buf.at[t, mine, y])
        for r in (1, 7, 2, 6, 3, 5, 4):
            gy[t, r].wait_recv()
            spread_x(t, buf.at[t, mine, lax.rem(y + NY - r, NY)])
        to_sibling(t, 0)
        for r in range(1, NX):
            sends.append(column_x(t, r))

    def gather_x(t, d):
        column_x(t, NX - d).wait_recv()
        to_sibling(t, d)

    def block_of(slot):
        return column((slot - 1) // 2, core if slot % 2 else 1 - core)

    def fetched(t, slot):
        if slot == 0:
            return (k_ref if t == KEYS else v_ref)[...]
        return buf[t, block_of(slot)].reshape(SEG, HEAD_DIM)

    def absorb(slot):
        kc = fetched(KEYS, slot)
        vc = fetched(VALUES, slot)
        rows = rows_of(slot)
        kt_ref[:, rows] = kc.T
        for h in range(GROUP):
            s = dot_t(kc, q_ref[:, h * HEAD_DIM : (h + 1) * HEAD_DIM]) * SCALE_LOG2
            if slot:
                s = jnp.concatenate(
                    [s[SUMM * i : SUMM * (i + 1)] + bias[block_of(slot) * NY + i] for i in range(NY)], 0
                )
            else:
                key_pos = lax.broadcasted_iota(jnp.int32, (SEG, SEG), 0)
                query_pos = lax.broadcasted_iota(jnp.int32, (SEG, SEG), 1)
                s = jnp.where(key_pos <= query_pos, s, HIDDEN)
            s_ref[h] = s
            top_ref[slot, h : h + 1] = jnp.max(fold(s, jnp.max), 0, keepdims=True)
        for h in range(GROUP):
            e = jnp.exp2(s_ref[h] - top_ref[slot, h : h + 1])
            dp = dot_t(vc, g_ref[:, h * HEAD_DIM : (h + 1) * HEAD_DIM])
            total_ref[slot, h : h + 1] = jnp.sum(fold(e, jnp.sum), 0, keepdims=True)
            delta_ref[slot, h : h + 1] = jnp.sum(fold(e * dp, jnp.sum), 0, keepdims=True)
            e_ref[rows, h * SEG : (h + 1) * SEG] = e.astype(BF)
            dp_ref[h, rows, :] = dp

    def mask_terms():
        own = order_ref[seg]
        for xc in range(2 * NX):
            for yy in range(NY):
                bias[xc * NY + yy] = jnp.where(order_ref[yy * 2 * NX + xc] < own, 0.0, HIDDEN)

    mask_terms()
    for copy in fetch[2:]:
        copy.wait()
    for h in range(GROUP):
        qs_ref[rows_of(h), :] = q_ref[:, h * HEAD_DIM : (h + 1) * HEAD_DIM]
        gs_ref[rows_of(h), :] = g_ref[:, h * HEAD_DIM : (h + 1) * HEAD_DIM]
    absorb(0)
    gather_y(KEYS)
    gather_y(VALUES)
    absorb(1)
    gs[KEYS, 0].wait_recv()
    gs[VALUES, 0].wait_recv()
    absorb(2)
    for d in (3, 1, 2):
        gather_x(KEYS, d)
    for d in (3, 1, 2):
        gather_x(VALUES, d)
        absorb(1 + 2 * d)
    for d in (3, 1, 2):
        gs[KEYS, d].wait_recv()
        gs[VALUES, d].wait_recv()
        absorb(2 + 2 * d)

    top = top_ref[0]
    for slot in range(1, CHUNKS):
        top = jnp.maximum(top, top_ref[slot])
    total = jnp.zeros((GROUP, SEG), F32)
    delta = jnp.zeros((GROUP, SEG), F32)
    for slot in range(CHUNKS):
        factor = jnp.exp2(top_ref[slot] - top)
        top_ref[slot] = factor
        total = total + factor * total_ref[slot]
        delta = delta + factor * delta_ref[slot]
    inv = 1.0 / total
    for slot in range(CHUNKS):
        top_ref[slot] = top_ref[slot] * inv
    delta_ref[0] = delta * inv

    my_cols = aligned(z, HEAD_DIM)
    my_rows = pl.ds(z * SUMM, SUMM)
    outs = (ok_ref, ov_ref)

    def terms(t, slot):
        if t == KEYS:
            return dot(ds_ref[rows_of(slot), :], qs_ref[...]) * SCALE
        return dot(e_ref[rows_of(slot), :], gs_ref[...])

    rs, rx, ry = {}, {}, {}

    def z_copy(t, r, src):
        return remote(src, outs[t].at[:, my_cols], z_s.at[t, r], z_r.at[t, r], z_dev(r))

    def early(t, r):
        return z_copy(t, r, local.at[t, pl.ds(lax.rem(z + r, NZ) * SUMM, SUMM), :])

    def normalise(slot):
        rows = rows_of(slot)
        for h in range(GROUP):
            wide = slice(h * SEG, (h + 1) * SEG)
            p = e_ref[rows, wide].astype(F32) * top_ref[slot, h : h + 1]
            e_ref[rows, wide] = p.astype(BF)
            ds_ref[rows, wide] = (p * (dp_ref[h, rows, :] - delta_ref[0, h : h + 1])).astype(BF)

    def reduce_x(t):
        def give(columns):
            for d in columns:
                sib_out[t, d] = split(terms(t, 2 + 2 * d)).astype(BF)
            for d in columns:
                rs[t, d] = go(remote(sib_out.at[t, d], sib_in.at[t, d], rs_s.at[t, d], rs_r.at[t, d], sibling))

        def take(columns):
            for d in columns:
                parts[d] = split(terms(t, 1 + 2 * d))
            for d in columns:
                rs[t, d].wait_recv()
                part = parts[d] + sib_in[t, d].astype(F32)
                if d:
                    x_out[t, d] = part.astype(BF)
                    rx[t, d] = go(
                        remote(x_out.at[t, d], x_in.at[t, d], rx_s.at[t, d], rx_r.at[t, d], x_dev(d))
                    )
                else:
                    x_own[t] = part

        give((2,))
        give((1, 3, 0))
        take((2,))
        take((1, 3))
        take((0,))
        part = terms(t, 0)
        local[t] = part.astype(BF)
        summ[t] = part[SEG - SUMM :]
        for r in range(1, NZ):

            @pl.when(lax.rem(z + r, NZ) != NZ - 1)
            def _(r=r):
                early(t, r).start()

    def reduce_y(t):
        acc = x_own[t]
        for d in (1, 3, 2):
            rx[t, d].wait_recv()
            acc = acc + x_in[t, d].astype(F32)
        x_own[t] = acc
        y_out[t] = acc.astype(BF)
        for r in FAR_FIRST:
            ry[t, r] = go(
                remote(y_out.at[t, lax.rem(y + r, NY)], y_in.at[t, r], ry_s.at[t, r], ry_r.at[t, r], y_dev(r))
            )

    def reduce_end(t):
        acc = x_own[t, y] + summ[t]
        for r in range(1, NY):
            ry[t, r].wait_recv()
            acc = acc + y_in[t, r].astype(F32)
        final[t] = acc.astype(BF)
        for r in range(1, NZ):

            @pl.when(lax.rem(z + r, NZ) == NZ - 1)
            def _(r=r):
                z_copy(t, r, final.at[t]).start()

        @pl.when(z != NZ - 1)
        def _():
            pltpu.make_async_copy(local.at[t, my_rows, :], outs[t].at[:, my_cols], own_sem.at[t]).start()

        @pl.when(z == NZ - 1)
        def _():
            pltpu.make_async_copy(final.at[t], outs[t].at[:, my_cols], own_sem.at[t]).start()

    def dq_cols(h):
        return aligned(z * GROUP + h, HEAD_DIM)

    def query_grads(first):
        for h in (first, first + 1):
            acc = dot(kt_ref[...], ds_ref[:, h * SEG : (h + 1) * SEG])
            dq_ref[h] = (acc * SCALE).T.astype(BF)
        for h in (first, first + 1):
            for r in FAR_FIRST:
                to = pl.ds(lax.rem(z + r, NZ) * SUMM, SUMM)
                remote(dq_ref.at[h, to, :], oq_ref.at[:, dq_cols(h)], q_s.at[r], q_r.at[r], z_dev(r)).start()

    for slot in range(CHUNKS):
        normalise(slot)
    query_grads(0)
    reduce_x(VALUES)
    query_grads(2)
    reduce_x(KEYS)
    query_grads(4)
    reduce_y(VALUES)
    query_grads(6)
    own_dq = [
        pltpu.make_async_copy(dq_ref.at[h, my_rows, :], oq_ref.at[:, dq_cols(h)], in_sem.at[h])
        for h in range(GROUP)
    ]
    for copy in own_dq:
        copy.start()
    reduce_y(KEYS)
    reduce_end(VALUES)
    reduce_end(KEYS)

    for copy in own_dq:
        copy.wait()
    oq_cols = aligned(z, GROUP * HEAD_DIM)
    for r in range(1, NZ):
        remote(oq_ref.at[:, oq_cols], oq_ref.at[:, oq_cols], q_s.at[r], q_r.at[r], z_dev(r)).wait()
    for t in (VALUES, KEYS):
        for r in range(1, NZ):
            early(t, r).wait()
        pltpu.make_async_copy(final.at[t], outs[t].at[:, my_cols], own_sem.at[t]).wait()
    for copy in sends:
        copy.wait_send()


def place(a_ref, b_ref, c_ref, oa_ref, ob_ref, oc_ref, mid, get_sem, put_sem):
    width = mid.shape[2]
    pieces = [(a_ref.at[:, pl.ds(i * width, width)], oa_ref.at[:, pl.ds(i * width, width)]) for i in range(8)]
    pieces += [(b_ref, ob_ref), (c_ref, oc_ref)]
    gets = [pltpu.make_async_copy(src, mid.at[i], get_sem.at[i]) for i, (src, _) in enumerate(pieces)]
    puts = [pltpu.make_async_copy(mid.at[i], dst, put_sem.at[i]) for i, (_, dst) in enumerate(pieces)]
    for copy in gets:
        copy.start()
    for get, put in zip(gets, puts):
        get.wait()
        put.start()
    for copy in puts:
        copy.wait()


def backward(queries, key_rows, value_rows, grad_out, seg_order):
    hbm = pl.BlockSpec(memory_space=pl.ANY)
    smem = pl.BlockSpec(memory_space=pltpu.SMEM)
    width = CHUNKS * SEG
    column = (NY, SUMM, HEAD_DIM)
    outs = [
        jax.ShapeDtypeStruct((SUMM, NZ * GROUP * HEAD_DIM), BF),
        jax.ShapeDtypeStruct((SUMM, NZ * HEAD_DIM), BF),
        jax.ShapeDtypeStruct((SUMM, NZ * HEAD_DIM), BF),
    ]
    scratch = [
        pltpu.SMEM((2 * NX * NY,), F32),
        pltpu.VMEM((SEG, GROUP * HEAD_DIM), BF),
        pltpu.VMEM((SEG, HEAD_DIM), BF),
        pltpu.VMEM((SEG, HEAD_DIM), BF),
        pltpu.VMEM((SEG, GROUP * HEAD_DIM), BF),
        pltpu.VMEM((2, 2 * NX) + column, BF),
        pltpu.VMEM((GROUP, SEG, SEG), F32),
        pltpu.VMEM((GROUP, width, SEG), F32),
        pltpu.VMEM((width, GROUP * SEG), BF),
        pltpu.VMEM((width, GROUP * SEG), BF),
        pltpu.VMEM((GROUP * SEG, HEAD_DIM), BF),
        pltpu.VMEM((GROUP * SEG, HEAD_DIM), BF),
        pltpu.VMEM((HEAD_DIM, width), BF),
        pltpu.VMEM((GROUP, SEG, HEAD_DIM), BF),
        pltpu.VMEM((CHUNKS, GROUP, SEG), F32),
        pltpu.VMEM((CHUNKS, GROUP, SEG), F32),
        pltpu.VMEM((CHUNKS, GROUP, SEG), F32),
        pltpu.VMEM((2, NX) + column, BF),
        pltpu.VMEM((2, NX) + column, BF),
        pltpu.VMEM((NX,) + column, F32),
        pltpu.VMEM((2, NX) + column, BF),
        pltpu.VMEM((2, NX) + column, BF),
        pltpu.VMEM((2,) + column, F32),
        pltpu.VMEM((2,) + column, BF),
        pltpu.VMEM((2,) + column, BF),
        pltpu.VMEM((2, SEG, HEAD_DIM), BF),
        pltpu.VMEM((2, SUMM, HEAD_DIM), F32),
        pltpu.VMEM((2, SUMM, HEAD_DIM), BF),
    ]
    pairs = [(2, NY), (2, NX), (2, NX), (2, NX), (2, NX), (2, NY), (NZ,), (2, NZ)]
    scratch += [pltpu.SemaphoreType.DMA((8,)), pltpu.SemaphoreType.DMA((2,))]
    scratch += [pltpu.SemaphoreType.DMA(shape) for shape in pairs for _ in range(2)]
    raw = pl.pallas_call(
        kernel,
        out_shape=outs,
        in_specs=[smem, hbm, hbm, hbm, hbm],
        out_specs=[hbm, hbm, hbm],
        scratch_shapes=scratch,
        compiler_params=pltpu.CompilerParams(
            collective_id=0, has_side_effects=True, vmem_limit_bytes=62 * 2**20
        ),
        name="attention_backward",
    )(seg_order, queries, key_rows, value_rows, grad_out)
    return pl.pallas_call(
        place,
        out_shape=outs,
        in_specs=[hbm, hbm, hbm],
        out_specs=[hbm, hbm, hbm],
        scratch_shapes=[
            pltpu.VMEM((10, SUMM, NZ * HEAD_DIM), BF),
            pltpu.SemaphoreType.DMA((10,)),
            pltpu.SemaphoreType.DMA((10,)),
        ],
        compiler_params=pltpu.CompilerParams(vmem_limit_bytes=62 * 2**20),
        name="place",
    )(*raw)


def solution(mesh):
    in_specs = (P("seg", "tp"), P("seg", "tp"), P("seg", "tp"), P("seg", "tp"), P())
    out_specs = (P(("seg", "tp"), None), P(("seg", "tp"), None), P(("seg", "tp"), None))
    return jax.shard_map(backward, mesh=mesh, in_specs=in_specs, out_specs=out_specs, check_vma=False)
```

```python
import jax
import jax.numpy as jnp
from jax import lax
from jax.experimental import pallas as pl
from jax.experimental.pallas import tpu as pltpu
from jax.sharding import PartitionSpec as P

HEAD_DIM = 128
SUMM = 32
SEG = 256
NY, NX, NZ = 8, 4, 8
GROUP = 8
CHUNKS = 9
SCALE = HEAD_DIM**-0.5
SCALE_LOG2 = SCALE * 1.4426950408889634
HIDDEN = -1e30
BF = jnp.bfloat16
F32 = jnp.float32
MESH = pl.DeviceIdType.MESH
KEYS, VALUES = 0, 1
FAR_FIRST = (4, 3, 5, 2, 6, 1, 7)


def dot(a, b):
    return jnp.dot(a, b, preferred_element_type=F32)


def dot_t(a, b):
    return lax.dot_general(a, b, (((1,), (1,)), ((), ())), preferred_element_type=F32)


def split(a):
    return a.reshape(NY, SUMM, HEAD_DIM)


def fold(a, op):
    return op(a.reshape(SEG // 8, 8, SEG), 0)


def rows_of(slot):
    return slice(slot * SEG, (slot + 1) * SEG)


def aligned(index, size):
    return pl.ds(pl.multiple_of(index * size, size), size)


def kernel(
    order_ref, q_hbm, k_hbm, v_hbm, g_hbm, oq_ref, ok_ref, ov_ref,
    bias, q_ref, k_ref, v_ref, g_ref, buf, s_ref, dp_ref, e_ref, ds_ref, qs_ref, gs_ref, kt_ref, dq_ref,
    top_ref, total_ref, delta_ref,
    sib_out, sib_in, parts, x_out, x_in, x_own, y_out, y_in, local, summ, final,
    in_sem, own_sem, gy_s, gy_r, gx_s, gx_r, gs_s, gs_r,
    rs_s, rs_r, rx_s, rx_r, ry_s, ry_r, q_s, q_r, z_s, z_r,
):
    seg = lax.axis_index("seg")
    z = lax.axis_index("tp")
    core = lax.rem(seg, 2)
    x = lax.rem(seg // 2, NX)
    y = seg // (2 * NX)

    def seg_dev(yy, xx, cc):
        return {"seg": (yy * NX + xx) * 2 + cc}

    def y_dev(r):
        return seg_dev(lax.rem(y + r, NY), x, core)

    def x_dev(r):
        return seg_dev(y, lax.rem(x + r, NX), core)

    def z_dev(r):
        return {"tp": lax.rem(z + r, NZ)}

    sibling = seg_dev(y, x, 1 - core)

    def column(d, cc):
        return lax.rem(x + d, NX) * 2 + cc

    def remote(src, dst, send, recv, dev):
        return pltpu.make_async_remote_copy(
            src_ref=src, dst_ref=dst, send_sem=send, recv_sem=recv, device_id=dev, device_id_type=MESH
        )

    mine = column(0, core)
    fetch = [
        pltpu.make_async_copy(k_hbm.at[pl.ds(SEG - SUMM, SUMM), :], buf.at[KEYS, mine, y], in_sem.at[0]),
        pltpu.make_async_copy(v_hbm.at[pl.ds(SEG - SUMM, SUMM), :], buf.at[VALUES, mine, y], in_sem.at[1]),
        pltpu.make_async_copy(k_hbm, k_ref, in_sem.at[2]),
        pltpu.make_async_copy(q_hbm, q_ref, in_sem.at[3]),
        pltpu.make_async_copy(v_hbm, v_ref, in_sem.at[4]),
        pltpu.make_async_copy(g_hbm, g_ref, in_sem.at[5]),
    ]
    for copy in fetch:
        copy.start()
    barrier = pltpu.get_barrier_semaphore()
    peers = [y_dev(r) for r in FAR_FIRST] + [x_dev(r) for r in range(1, NX)]
    peers += [sibling] + [z_dev(r) for r in range(1, NZ)]
    for dev in peers:
        pl.semaphore_signal(barrier, inc=1, device_id=dev, device_id_type=MESH)
    sends = []

    def go(copy):
        copy.start()
        sends.append(copy)
        return copy

    fetch[0].wait()
    fetch[1].wait()
    pl.semaphore_wait(barrier, len(peers))

    gy, gs = {}, {}
    for t in (KEYS, VALUES):
        for r in FAR_FIRST:
            gy[t, r] = go(
                remote(buf.at[t, mine, y], buf.at[t, mine, y], gy_s.at[t, r], gy_r.at[t, r], y_dev(r))
            )

    def spread_x(t, block):
        for r in (1, 3):
            remote(block, block, gx_s.at[t, r], gx_r.at[t, r], x_dev(r)).start()

    def column_x(t, r):
        block = buf.at[t, mine]
        return remote(block, block, gx_s.at[t, r], gx_r.at[t, r], x_dev(r))

    def to_sibling(t, d):
        block = buf.at[t, column(d, core)]
        gs[t, d] = go(remote(block, block, gs_s.at[t, d], gs_r.at[t, d], sibling))

    def gather_y(t):
        for r in (1, 7, 2, 6, 3, 5, 4):
            gy[t, r].wait_recv()
            spread_x(t, buf.at[t, mine, lax.rem(y + NY - r, NY)])
        to_sibling(t, 0)

    def gather_x(t, d):
        column_x(t, NX - d).wait_recv()
        to_sibling(t, d)

    for t in (KEYS, VALUES):
        spread_x(t, buf.at[t, mine, y])

    def block_of(slot):
        return column((slot - 1) // 2, core if slot % 2 else 1 - core)

    def fetched(t, slot):
        if slot == 0:
            return (k_ref if t == KEYS else v_ref)[...]
        return buf[t, block_of(slot)].reshape(SEG, HEAD_DIM)

    def absorb(slot):
        kc = fetched(KEYS, slot)
        vc = fetched(VALUES, slot)
        rows = rows_of(slot)
        kt_ref[:, rows] = kc.T
        for h in range(GROUP):
            s = dot_t(kc, q_ref[:, h * HEAD_DIM : (h + 1) * HEAD_DIM]) * SCALE_LOG2
            if slot:
                s = jnp.concatenate(
                    [s[SUMM * i : SUMM * (i + 1)] + bias[block_of(slot) * NY + i] for i in range(NY)], 0
                )
            else:
                key_pos = lax.broadcasted_iota(jnp.int32, (SEG, SEG), 0)
                query_pos = lax.broadcasted_iota(jnp.int32, (SEG, SEG), 1)
                s = jnp.where(key_pos <= query_pos, s, HIDDEN)
            s_ref[h] = s
            top_ref[slot, h : h + 1] = jnp.max(fold(s, jnp.max), 0, keepdims=True)
        for h in range(GROUP):
            e = jnp.exp2(s_ref[h] - top_ref[slot, h : h + 1])
            dp = dot_t(vc, g_ref[:, h * HEAD_DIM : (h + 1) * HEAD_DIM])
            total_ref[slot, h : h + 1] = jnp.sum(fold(e, jnp.sum), 0, keepdims=True)
            delta_ref[slot, h : h + 1] = jnp.sum(fold(e * dp, jnp.sum), 0, keepdims=True)
            e_ref[rows, h * SEG : (h + 1) * SEG] = e.astype(BF)
            dp_ref[h, rows, :] = dp

    def mask_terms():
        own = order_ref[seg]
        for xc in range(2 * NX):
            for yy in range(NY):
                bias[xc * NY + yy] = jnp.where(order_ref[yy * 2 * NX + xc] < own, 0.0, HIDDEN)

    mask_terms()
    for copy in fetch[2:]:
        copy.wait()
    for h in range(GROUP):
        qs_ref[rows_of(h), :] = q_ref[:, h * HEAD_DIM : (h + 1) * HEAD_DIM]
        gs_ref[rows_of(h), :] = g_ref[:, h * HEAD_DIM : (h + 1) * HEAD_DIM]
    absorb(0)
    gather_y(KEYS)
    gather_y(VALUES)
    for t in (KEYS, VALUES):
        column_x(t, 2).start()
        for r in range(1, NX):
            sends.append(column_x(t, r))
    absorb(1)
    gs[KEYS, 0].wait_recv()
    gs[VALUES, 0].wait_recv()
    absorb(2)
    for t in (KEYS, VALUES):
        for d in (3, 1):
            gather_x(t, d)

    def absorb_sibling(d):
        gs[KEYS, d].wait_recv()
        gs[VALUES, d].wait_recv()
        absorb(2 + 2 * d)

    absorb(7)
    absorb(3)
    absorb_sibling(3)
    for t in (KEYS, VALUES):
        gather_x(t, 2)
    absorb_sibling(1)
    absorb(5)
    absorb_sibling(2)

    top = top_ref[0]
    for slot in range(1, CHUNKS):
        top = jnp.maximum(top, top_ref[slot])
    total = jnp.zeros((GROUP, SEG), F32)
    delta = jnp.zeros((GROUP, SEG), F32)
    for slot in range(CHUNKS):
        factor = jnp.exp2(top_ref[slot] - top)
        top_ref[slot] = factor
        total = total + factor * total_ref[slot]
        delta = delta + factor * delta_ref[slot]
    inv = 1.0 / total
    for slot in range(CHUNKS):
        top_ref[slot] = top_ref[slot] * inv
    delta_ref[0] = delta * inv

    my_cols = aligned(z, HEAD_DIM)
    my_rows = pl.ds(z * SUMM, SUMM)
    outs = (ok_ref, ov_ref)

    def terms(t, slot):
        if t == KEYS:
            return dot(ds_ref[rows_of(slot), :], qs_ref[...]) * SCALE
        return dot(e_ref[rows_of(slot), :], gs_ref[...])

    rs, rx, ry = {}, {}, {}

    def z_copy(t, r, src):
        return remote(src, outs[t].at[:, my_cols], z_s.at[t, r], z_r.at[t, r], z_dev(r))

    def early(t, r):
        return z_copy(t, r, local.at[t, pl.ds(lax.rem(z + r, NZ) * SUMM, SUMM), :])

    def normalise(slot):
        rows = rows_of(slot)
        for h in range(GROUP):
            wide = slice(h * SEG, (h + 1) * SEG)
            p = e_ref[rows, wide].astype(F32) * top_ref[slot, h : h + 1]
            e_ref[rows, wide] = p.astype(BF)
            ds_ref[rows, wide] = (p * (dp_ref[h, rows, :] - delta_ref[0, h : h + 1])).astype(BF)

    def give(t, columns):
        for d in columns:
            sib_out[t, d] = split(terms(t, 2 + 2 * d)).astype(BF)
        for d in columns:
            rs[t, d] = go(remote(sib_out.at[t, d], sib_in.at[t, d], rs_s.at[t, d], rs_r.at[t, d], sibling))

    def take(t, columns):
        for d in columns:
            parts[d] = split(terms(t, 1 + 2 * d))
        for d in columns:
            rs[t, d].wait_recv()
            part = parts[d] + sib_in[t, d].astype(F32)
            if d:
                x_out[t, d] = part.astype(BF)
                rx[t, d] = go(remote(x_out.at[t, d], x_in.at[t, d], rx_s.at[t, d], rx_r.at[t, d], x_dev(d)))
            else:
                x_own[t] = part

    def reduce_x(t):
        give(t, (2,))
        give(t, (1, 3))
        take(t, (2,))
        take(t, (1, 3))

    def reduce_own(t):
        give(t, (0,))
        part = terms(t, 0)
        take(t, (0,))
        local[t] = part.astype(BF)
        summ[t] = part[SEG - SUMM :]
        for r in range(1, NZ):

            @pl.when(lax.rem(z + r, NZ) != NZ - 1)
            def _(r=r):
                early(t, r).start()

    def reduce_y(t):
        acc = x_own[t]
        for d in (1, 3, 2):
            rx[t, d].wait_recv()
            acc = acc + x_in[t, d].astype(F32)
        x_own[t] = acc
        y_out[t] = acc.astype(BF)
        for r in FAR_FIRST:
            ry[t, r] = go(
                remote(y_out.at[t, lax.rem(y + r, NY)], y_in.at[t, r], ry_s.at[t, r], ry_r.at[t, r], y_dev(r))
            )

    def reduce_end(t):
        acc = x_own[t, y] + summ[t]
        for r in range(1, NY):
            ry[t, r].wait_recv()
            acc = acc + y_in[t, r].astype(F32)
        final[t] = acc.astype(BF)
        for r in range(1, NZ):

            @pl.when(lax.rem(z + r, NZ) == NZ - 1)
            def _(r=r):
                z_copy(t, r, final.at[t]).start()

        @pl.when(z != NZ - 1)
        def _():
            pltpu.make_async_copy(local.at[t, my_rows, :], outs[t].at[:, my_cols], own_sem.at[t]).start()

        @pl.when(z == NZ - 1)
        def _():
            pltpu.make_async_copy(final.at[t], outs[t].at[:, my_cols], own_sem.at[t]).start()

    def dq_cols(h):
        return aligned(z * GROUP + h, HEAD_DIM)

    def query_grads(first):
        for h in (first, first + 1):
            acc = dot(kt_ref[...], ds_ref[:, h * SEG : (h + 1) * SEG])
            dq_ref[h] = (acc * SCALE).T.astype(BF)
        for h in (first, first + 1):
            for r in FAR_FIRST:
                to = pl.ds(lax.rem(z + r, NZ) * SUMM, SUMM)
                remote(dq_ref.at[h, to, :], oq_ref.at[:, dq_cols(h)], q_s.at[r], q_r.at[r], z_dev(r)).start()

    for slot in range(CHUNKS):
        normalise(slot)
    query_grads(0)
    query_grads(2)
    reduce_x(VALUES)
    query_grads(4)
    reduce_x(KEYS)
    query_grads(6)
    reduce_own(VALUES)
    reduce_own(KEYS)
    reduce_y(VALUES)
    reduce_y(KEYS)
    own_dq = [
        pltpu.make_async_copy(dq_ref.at[h, my_rows, :], oq_ref.at[:, dq_cols(h)], in_sem.at[h])
        for h in range(GROUP)
    ]
    for copy in own_dq:
        copy.start()
    reduce_end(VALUES)
    reduce_end(KEYS)

    for copy in own_dq:
        copy.wait()
    oq_cols = aligned(z, GROUP * HEAD_DIM)
    for r in range(1, NZ):
        remote(oq_ref.at[:, oq_cols], oq_ref.at[:, oq_cols], q_s.at[r], q_r.at[r], z_dev(r)).wait()
    for t in (VALUES, KEYS):
        for r in range(1, NZ):
            early(t, r).wait()
        pltpu.make_async_copy(final.at[t], outs[t].at[:, my_cols], own_sem.at[t]).wait()
    for copy in sends:
        copy.wait_send()


def place(a_ref, b_ref, c_ref, oa_ref, ob_ref, oc_ref, mid, get_sem, put_sem):
    width = mid.shape[2]
    pieces = [(a_ref.at[:, pl.ds(i * width, width)], oa_ref.at[:, pl.ds(i * width, width)]) for i in range(8)]
    pieces += [(b_ref, ob_ref), (c_ref, oc_ref)]
    gets = [pltpu.make_async_copy(src, mid.at[i], get_sem.at[i]) for i, (src, _) in enumerate(pieces)]
    puts = [pltpu.make_async_copy(mid.at[i], dst, put_sem.at[i]) for i, (_, dst) in enumerate(pieces)]
    for copy in gets:
        copy.start()
    for get, put in zip(gets, puts):
        get.wait()
        put.start()
    for copy in puts:
        copy.wait()


def backward(queries, key_rows, value_rows, grad_out, seg_order):
    hbm = pl.BlockSpec(memory_space=pl.ANY)
    smem = pl.BlockSpec(memory_space=pltpu.SMEM)
    width = CHUNKS * SEG
    column = (NY, SUMM, HEAD_DIM)
    outs = [
        jax.ShapeDtypeStruct((SUMM, NZ * GROUP * HEAD_DIM), BF),
        jax.ShapeDtypeStruct((SUMM, NZ * HEAD_DIM), BF),
        jax.ShapeDtypeStruct((SUMM, NZ * HEAD_DIM), BF),
    ]
    scratch = [
        pltpu.SMEM((2 * NX * NY,), F32),
        pltpu.VMEM((SEG, GROUP * HEAD_DIM), BF),
        pltpu.VMEM((SEG, HEAD_DIM), BF),
        pltpu.VMEM((SEG, HEAD_DIM), BF),
        pltpu.VMEM((SEG, GROUP * HEAD_DIM), BF),
        pltpu.VMEM((2, 2 * NX) + column, BF),
        pltpu.VMEM((GROUP, SEG, SEG), F32),
        pltpu.VMEM((GROUP, width, SEG), F32),
        pltpu.VMEM((width, GROUP * SEG), BF),
        pltpu.VMEM((width, GROUP * SEG), BF),
        pltpu.VMEM((GROUP * SEG, HEAD_DIM), BF),
        pltpu.VMEM((GROUP * SEG, HEAD_DIM), BF),
        pltpu.VMEM((HEAD_DIM, width), BF),
        pltpu.VMEM((GROUP, SEG, HEAD_DIM), BF),
        pltpu.VMEM((CHUNKS, GROUP, SEG), F32),
        pltpu.VMEM((CHUNKS, GROUP, SEG), F32),
        pltpu.VMEM((CHUNKS, GROUP, SEG), F32),
        pltpu.VMEM((2, NX) + column, BF),
        pltpu.VMEM((2, NX) + column, BF),
        pltpu.VMEM((NX,) + column, F32),
        pltpu.VMEM((2, NX) + column, BF),
        pltpu.VMEM((2, NX) + column, BF),
        pltpu.VMEM((2,) + column, F32),
        pltpu.VMEM((2,) + column, BF),
        pltpu.VMEM((2,) + column, BF),
        pltpu.VMEM((2, SEG, HEAD_DIM), BF),
        pltpu.VMEM((2, SUMM, HEAD_DIM), F32),
        pltpu.VMEM((2, SUMM, HEAD_DIM), BF),
    ]
    pairs = [(2, NY), (2, NX), (2, NX), (2, NX), (2, NX), (2, NY), (NZ,), (2, NZ)]
    scratch += [pltpu.SemaphoreType.DMA((8,)), pltpu.SemaphoreType.DMA((2,))]
    scratch += [pltpu.SemaphoreType.DMA(shape) for shape in pairs for _ in range(2)]
    raw = pl.pallas_call(
        kernel,
        out_shape=outs,
        in_specs=[smem, hbm, hbm, hbm, hbm],
        out_specs=[hbm, hbm, hbm],
        scratch_shapes=scratch,
        compiler_params=pltpu.CompilerParams(
            collective_id=0, has_side_effects=True, vmem_limit_bytes=62 * 2**20
        ),
        name="attention_backward",
    )(seg_order, queries, key_rows, value_rows, grad_out)
    return pl.pallas_call(
        place,
        out_shape=outs,
        in_specs=[hbm, hbm, hbm],
        out_specs=[hbm, hbm, hbm],
        scratch_shapes=[
            pltpu.VMEM((10, SUMM, NZ * HEAD_DIM), BF),
            pltpu.SemaphoreType.DMA((10,)),
            pltpu.SemaphoreType.DMA((10,)),
        ],
        compiler_params=pltpu.CompilerParams(vmem_limit_bytes=62 * 2**20),
        name="place",
    )(*raw)


def solution(mesh):
    in_specs = (P("seg", "tp"), P("seg", "tp"), P("seg", "tp"), P("seg", "tp"), P())
    out_specs = (P(("seg", "tp"), None), P(("seg", "tp"), None), P(("seg", "tp"), None))
    return jax.shard_map(backward, mesh=mesh, in_specs=in_specs, out_specs=out_specs, check_vma=False)
```

```python
import jax
import jax.numpy as jnp
from jax import lax
from jax.experimental import pallas as pl
from jax.experimental.pallas import tpu as pltpu
from jax.sharding import PartitionSpec as P

HEAD_DIM = 128
SUMM = 32
SEG = 256
NY, NX, NZ = 8, 4, 8
GROUP = 8
CHUNKS = 9
SCALE = HEAD_DIM**-0.5
SCALE_LOG2 = SCALE * 1.4426950408889634
HIDDEN = -1e30
BF = jnp.bfloat16
F32 = jnp.float32
MESH = pl.DeviceIdType.MESH
KEYS, VALUES = 0, 1
FAR_FIRST = (4, 3, 5, 2, 6, 1, 7)


def dot(a, b):
    return jnp.dot(a, b, preferred_element_type=F32)


def dot_t(a, b):
    return lax.dot_general(a, b, (((1,), (1,)), ((), ())), preferred_element_type=F32)


def split(a):
    return a.reshape(NY, SUMM, HEAD_DIM)


def fold(a, op):
    return op(a.reshape(SEG // 8, 8, SEG), 0)


def rows_of(slot):
    return slice(slot * SEG, (slot + 1) * SEG)


def aligned(index, size):
    return pl.ds(pl.multiple_of(index * size, size), size)


def kernel(
    order_ref, q_hbm, k_hbm, v_hbm, g_hbm, oq_ref, ok_ref, ov_ref,
    bias, q_ref, k_ref, v_ref, g_ref, buf, s_ref, dp_ref, e_ref, ds_ref, qs_ref, gs_ref, kt_ref, dq_ref,
    top_ref, total_ref, delta_ref,
    sib_out, sib_in, parts, x_out, x_in, x_own, y_out, y_in, local, summ, final,
    in_sem, own_sem, gy_s, gy_r, gx_s, gx_r, gs_s, gs_r,
    rs_s, rs_r, rx_s, rx_r, ry_s, ry_r, q_s, q_r, z_s, z_r,
):
    seg = lax.axis_index("seg")
    z = lax.axis_index("tp")
    core = lax.rem(seg, 2)
    x = lax.rem(seg // 2, NX)
    y = seg // (2 * NX)

    def seg_dev(yy, xx, cc):
        return {"seg": (yy * NX + xx) * 2 + cc}

    def y_dev(r):
        return seg_dev(lax.rem(y + r, NY), x, core)

    def x_dev(r):
        return seg_dev(y, lax.rem(x + r, NX), core)

    def z_dev(r):
        return {"tp": lax.rem(z + r, NZ)}

    sibling = seg_dev(y, x, 1 - core)

    def column(d, cc):
        return lax.rem(x + d, NX) * 2 + cc

    def remote(src, dst, send, recv, dev):
        return pltpu.make_async_remote_copy(
            src_ref=src, dst_ref=dst, send_sem=send, recv_sem=recv, device_id=dev, device_id_type=MESH
        )

    mine = column(0, core)
    fetch = [
        pltpu.make_async_copy(k_hbm.at[pl.ds(SEG - SUMM, SUMM), :], buf.at[KEYS, mine, y], in_sem.at[0]),
        pltpu.make_async_copy(v_hbm.at[pl.ds(SEG - SUMM, SUMM), :], buf.at[VALUES, mine, y], in_sem.at[1]),
        pltpu.make_async_copy(k_hbm, k_ref, in_sem.at[2]),
        pltpu.make_async_copy(q_hbm, q_ref, in_sem.at[3]),
        pltpu.make_async_copy(v_hbm, v_ref, in_sem.at[4]),
        pltpu.make_async_copy(g_hbm, g_ref, in_sem.at[5]),
    ]
    for copy in fetch:
        copy.start()
    barrier = pltpu.get_barrier_semaphore()
    peers = [y_dev(r) for r in FAR_FIRST] + [x_dev(r) for r in range(1, NX)]
    peers += [sibling] + [z_dev(r) for r in range(1, NZ)]
    for dev in peers:
        pl.semaphore_signal(barrier, inc=1, device_id=dev, device_id_type=MESH)
    sends = []

    def go(copy):
        copy.start()
        sends.append(copy)
        return copy

    fetch[0].wait()
    fetch[1].wait()
    pl.semaphore_wait(barrier, len(peers))

    gy, gs = {}, {}
    for t in (KEYS, VALUES):
        for r in FAR_FIRST:
            gy[t, r] = go(
                remote(buf.at[t, mine, y], buf.at[t, mine, y], gy_s.at[t, r], gy_r.at[t, r], y_dev(r))
            )

    def spread_x(t, block):
        for r in (1, 3):
            remote(block, block, gx_s.at[t, r], gx_r.at[t, r], x_dev(r)).start()

    def column_x(t, r):
        block = buf.at[t, mine]
        return remote(block, block, gx_s.at[t, r], gx_r.at[t, r], x_dev(r))

    def to_sibling(t, d):
        block = buf.at[t, column(d, core)]
        gs[t, d] = go(remote(block, block, gs_s.at[t, d], gs_r.at[t, d], sibling))

    def gather_y(t):
        for r in (1, 7, 2, 6, 3, 5, 4):
            gy[t, r].wait_recv()
            spread_x(t, buf.at[t, mine, lax.rem(y + NY - r, NY)])
        to_sibling(t, 0)

    def gather_x(t, d):
        column_x(t, NX - d).wait_recv()
        to_sibling(t, d)

    for t in (KEYS, VALUES):
        spread_x(t, buf.at[t, mine, y])

    def block_of(slot):
        return column((slot - 1) // 2, core if slot % 2 else 1 - core)

    def fetched(t, slot):
        if slot == 0:
            return (k_ref if t == KEYS else v_ref)[...]
        return buf[t, block_of(slot)].reshape(SEG, HEAD_DIM)

    def absorb(slot):
        kc = fetched(KEYS, slot)
        vc = fetched(VALUES, slot)
        rows = rows_of(slot)
        kt_ref[:, rows] = kc.T
        for h in range(GROUP):
            s = dot_t(kc, q_ref[:, h * HEAD_DIM : (h + 1) * HEAD_DIM]) * SCALE_LOG2
            if slot:
                s = jnp.concatenate(
                    [s[SUMM * i : SUMM * (i + 1)] + bias[block_of(slot) * NY + i] for i in range(NY)], 0
                )
            else:
                key_pos = lax.broadcasted_iota(jnp.int32, (SEG, SEG), 0)
                query_pos = lax.broadcasted_iota(jnp.int32, (SEG, SEG), 1)
                s = jnp.where(key_pos <= query_pos, s, HIDDEN)
            s_ref[h] = s
            top_ref[slot, h : h + 1] = jnp.max(fold(s, jnp.max), 0, keepdims=True)
        for h in range(GROUP):
            e = jnp.exp2(s_ref[h] - top_ref[slot, h : h + 1])
            dp = dot_t(vc, g_ref[:, h * HEAD_DIM : (h + 1) * HEAD_DIM])
            total_ref[slot, h : h + 1] = jnp.sum(fold(e, jnp.sum), 0, keepdims=True)
            delta_ref[slot, h : h + 1] = jnp.sum(fold(e * dp, jnp.sum), 0, keepdims=True)
            e_ref[rows, h * SEG : (h + 1) * SEG] = e.astype(BF)
            dp_ref[h, rows, :] = dp

    def mask_terms():
        own = order_ref[seg]
        for xc in range(2 * NX):
            for yy in range(NY):
                bias[xc * NY + yy] = jnp.where(order_ref[yy * 2 * NX + xc] < own, 0.0, HIDDEN)

    mask_terms()
    for copy in fetch[2:]:
        copy.wait()
    for h in range(GROUP):
        qs_ref[rows_of(h), :] = q_ref[:, h * HEAD_DIM : (h + 1) * HEAD_DIM]
        gs_ref[rows_of(h), :] = g_ref[:, h * HEAD_DIM : (h + 1) * HEAD_DIM]
    absorb(0)
    gather_y(KEYS)
    gather_y(VALUES)
    for t in (KEYS, VALUES):
        column_x(t, 2).start()
        for r in range(1, NX):
            sends.append(column_x(t, r))
    absorb(1)
    gs[KEYS, 0].wait_recv()
    gs[VALUES, 0].wait_recv()
    absorb(2)
    for t in (KEYS, VALUES):
        for d in (3, 1):
            gather_x(t, d)

    def absorb_sibling(d):
        gs[KEYS, d].wait_recv()
        gs[VALUES, d].wait_recv()
        absorb(2 + 2 * d)

    absorb(7)
    absorb(3)
    absorb_sibling(3)
    for t in (KEYS, VALUES):
        gather_x(t, 2)
    absorb_sibling(1)
    absorb(5)
    absorb_sibling(2)

    top = top_ref[0]
    for slot in range(1, CHUNKS):
        top = jnp.maximum(top, top_ref[slot])
    total = jnp.zeros((GROUP, SEG), F32)
    delta = jnp.zeros((GROUP, SEG), F32)
    for slot in range(CHUNKS):
        factor = jnp.exp2(top_ref[slot] - top)
        top_ref[slot] = factor
        total = total + factor * total_ref[slot]
        delta = delta + factor * delta_ref[slot]
    inv = 1.0 / total
    for slot in range(CHUNKS):
        top_ref[slot] = top_ref[slot] * inv
    delta_ref[0] = delta * inv

    my_cols = aligned(z, HEAD_DIM)
    my_rows = pl.ds(z * SUMM, SUMM)
    outs = (ok_ref, ov_ref)

    def terms(t, slot):
        if t == KEYS:
            return dot(ds_ref[rows_of(slot), :], qs_ref[...]) * SCALE
        return dot(e_ref[rows_of(slot), :], gs_ref[...])

    rs, rx, ry = {}, {}, {}

    def z_copy(t, r, src):
        return remote(src, outs[t].at[:, my_cols], z_s.at[t, r], z_r.at[t, r], z_dev(r))

    def early(t, r):
        return z_copy(t, r, local.at[t, pl.ds(lax.rem(z + r, NZ) * SUMM, SUMM), :])

    def normalise(slot):
        rows = rows_of(slot)
        for h in range(GROUP):
            wide = slice(h * SEG, (h + 1) * SEG)
            p = e_ref[rows, wide].astype(F32) * top_ref[slot, h : h + 1]
            e_ref[rows, wide] = p.astype(BF)
            ds_ref[rows, wide] = (p * (dp_ref[h, rows, :] - delta_ref[0, h : h + 1])).astype(BF)

    def give(t, columns):
        for d in columns:
            sib_out[t, d] = split(terms(t, 2 + 2 * d)).astype(BF)
        for d in columns:
            rs[t, d] = go(remote(sib_out.at[t, d], sib_in.at[t, d], rs_s.at[t, d], rs_r.at[t, d], sibling))

    def take(t, columns):
        for d in columns:
            parts[d] = split(terms(t, 1 + 2 * d))
        for d in columns:
            rs[t, d].wait_recv()
            part = parts[d] + sib_in[t, d].astype(F32)
            if d:
                x_out[t, d] = part.astype(BF)
                rx[t, d] = go(remote(x_out.at[t, d], x_in.at[t, d], rx_s.at[t, d], rx_r.at[t, d], x_dev(d)))
            else:
                x_own[t] = part

    def reduce_x(t):
        give(t, (2,))
        give(t, (1, 3))
        take(t, (2,))
        take(t, (1, 3))

    def reduce_own(t):
        give(t, (0,))
        part = terms(t, 0)
        take(t, (0,))
        local[t] = part.astype(BF)
        summ[t] = part[SEG - SUMM :]
        for r in range(1, NZ):

            @pl.when(lax.rem(z + r, NZ) != NZ - 1)
            def _(r=r):
                early(t, r).start()

    def reduce_y(t):
        acc = x_own[t]
        for d in (1, 3, 2):
            rx[t, d].wait_recv()
            acc = acc + x_in[t, d].astype(F32)
        x_own[t] = acc
        y_out[t] = acc.astype(BF)
        for r in FAR_FIRST:
            ry[t, r] = go(
                remote(y_out.at[t, lax.rem(y + r, NY)], y_in.at[t, r], ry_s.at[t, r], ry_r.at[t, r], y_dev(r))
            )

    def reduce_end(t):
        acc = x_own[t, y] + summ[t]
        for r in range(1, NY):
            ry[t, r].wait_recv()
            acc = acc + y_in[t, r].astype(F32)
        final[t] = acc.astype(BF)
        for r in range(1, NZ):

            @pl.when(lax.rem(z + r, NZ) == NZ - 1)
            def _(r=r):
                z_copy(t, r, final.at[t]).start()

        @pl.when(z != NZ - 1)
        def _():
            pltpu.make_async_copy(local.at[t, my_rows, :], outs[t].at[:, my_cols], own_sem.at[t]).start()

        @pl.when(z == NZ - 1)
        def _():
            pltpu.make_async_copy(final.at[t], outs[t].at[:, my_cols], own_sem.at[t]).start()

    def dq_cols(h):
        return aligned(z * GROUP + h, HEAD_DIM)

    def query_grads(first):
        for h in (first, first + 1):
            acc = dot(kt_ref[...], ds_ref[:, h * SEG : (h + 1) * SEG])
            dq_ref[h] = (acc * SCALE).T.astype(BF)
        for h in (first, first + 1):
            for r in FAR_FIRST:
                to = pl.ds(lax.rem(z + r, NZ) * SUMM, SUMM)
                remote(dq_ref.at[h, to, :], oq_ref.at[:, dq_cols(h)], q_s.at[r], q_r.at[r], z_dev(r)).start()

    for slot in range(CHUNKS):
        normalise(slot)
    query_grads(0)
    query_grads(2)
    reduce_x(VALUES)
    query_grads(4)
    reduce_x(KEYS)
    query_grads(6)
    reduce_own(VALUES)
    reduce_y(VALUES)
    reduce_own(KEYS)
    reduce_y(KEYS)
    own_dq = [
        pltpu.make_async_copy(dq_ref.at[h, my_rows, :], oq_ref.at[:, dq_cols(h)], in_sem.at[h])
        for h in range(GROUP)
    ]
    for copy in own_dq:
        copy.start()
    reduce_end(VALUES)
    reduce_end(KEYS)

    for copy in own_dq:
        copy.wait()
    oq_cols = aligned(z, GROUP * HEAD_DIM)
    for r in range(1, NZ):
        remote(oq_ref.at[:, oq_cols], oq_ref.at[:, oq_cols], q_s.at[r], q_r.at[r], z_dev(r)).wait()
    for t in (VALUES, KEYS):
        for r in range(1, NZ):
            early(t, r).wait()
        pltpu.make_async_copy(final.at[t], outs[t].at[:, my_cols], own_sem.at[t]).wait()
    for copy in sends:
        copy.wait_send()


def place(a_ref, b_ref, c_ref, oa_ref, ob_ref, oc_ref, mid, get_sem, put_sem):
    width = mid.shape[2]
    pieces = [(a_ref.at[:, pl.ds(i * width, width)], oa_ref.at[:, pl.ds(i * width, width)]) for i in range(8)]
    pieces += [(b_ref, ob_ref), (c_ref, oc_ref)]
    gets = [pltpu.make_async_copy(src, mid.at[i], get_sem.at[i]) for i, (src, _) in enumerate(pieces)]
    puts = [pltpu.make_async_copy(mid.at[i], dst, put_sem.at[i]) for i, (_, dst) in enumerate(pieces)]
    for copy in gets:
        copy.start()
    for get, put in zip(gets, puts):
        get.wait()
        put.start()
    for copy in puts:
        copy.wait()


def backward(queries, key_rows, value_rows, grad_out, seg_order):
    hbm = pl.BlockSpec(memory_space=pl.ANY)
    smem = pl.BlockSpec(memory_space=pltpu.SMEM)
    width = CHUNKS * SEG
    column = (NY, SUMM, HEAD_DIM)
    outs = [
        jax.ShapeDtypeStruct((SUMM, NZ * GROUP * HEAD_DIM), BF),
        jax.ShapeDtypeStruct((SUMM, NZ * HEAD_DIM), BF),
        jax.ShapeDtypeStruct((SUMM, NZ * HEAD_DIM), BF),
    ]
    scratch = [
        pltpu.SMEM((2 * NX * NY,), F32),
        pltpu.VMEM((SEG, GROUP * HEAD_DIM), BF),
        pltpu.VMEM((SEG, HEAD_DIM), BF),
        pltpu.VMEM((SEG, HEAD_DIM), BF),
        pltpu.VMEM((SEG, GROUP * HEAD_DIM), BF),
        pltpu.VMEM((2, 2 * NX) + column, BF),
        pltpu.VMEM((GROUP, SEG, SEG), F32),
        pltpu.VMEM((GROUP, width, SEG), F32),
        pltpu.VMEM((width, GROUP * SEG), BF),
        pltpu.VMEM((width, GROUP * SEG), BF),
        pltpu.VMEM((GROUP * SEG, HEAD_DIM), BF),
        pltpu.VMEM((GROUP * SEG, HEAD_DIM), BF),
        pltpu.VMEM((HEAD_DIM, width), BF),
        pltpu.VMEM((GROUP, SEG, HEAD_DIM), BF),
        pltpu.VMEM((CHUNKS, GROUP, SEG), F32),
        pltpu.VMEM((CHUNKS, GROUP, SEG), F32),
        pltpu.VMEM((CHUNKS, GROUP, SEG), F32),
        pltpu.VMEM((2, NX) + column, BF),
        pltpu.VMEM((2, NX) + column, BF),
        pltpu.VMEM((NX,) + column, F32),
        pltpu.VMEM((2, NX) + column, BF),
        pltpu.VMEM((2, NX) + column, BF),
        pltpu.VMEM((2,) + column, F32),
        pltpu.VMEM((2,) + column, BF),
        pltpu.VMEM((2,) + column, BF),
        pltpu.VMEM((2, SEG, HEAD_DIM), BF),
        pltpu.VMEM((2, SUMM, HEAD_DIM), F32),
        pltpu.VMEM((2, SUMM, HEAD_DIM), BF),
    ]
    pairs = [(2, NY), (2, NX), (2, NX), (2, NX), (2, NX), (2, NY), (NZ,), (2, NZ)]
    scratch += [pltpu.SemaphoreType.DMA((8,)), pltpu.SemaphoreType.DMA((2,))]
    scratch += [pltpu.SemaphoreType.DMA(shape) for shape in pairs for _ in range(2)]
    raw = pl.pallas_call(
        kernel,
        out_shape=outs,
        in_specs=[smem, hbm, hbm, hbm, hbm],
        out_specs=[hbm, hbm, hbm],
        scratch_shapes=scratch,
        compiler_params=pltpu.CompilerParams(
            collective_id=0, has_side_effects=True, vmem_limit_bytes=62 * 2**20
        ),
        name="attention_backward",
    )(seg_order, queries, key_rows, value_rows, grad_out)
    return pl.pallas_call(
        place,
        out_shape=outs,
        in_specs=[hbm, hbm, hbm],
        out_specs=[hbm, hbm, hbm],
        scratch_shapes=[
            pltpu.VMEM((10, SUMM, NZ * HEAD_DIM), BF),
            pltpu.SemaphoreType.DMA((10,)),
            pltpu.SemaphoreType.DMA((10,)),
        ],
        compiler_params=pltpu.CompilerParams(vmem_limit_bytes=62 * 2**20),
        name="place",
    )(*raw)


def solution(mesh):
    in_specs = (P("seg", "tp"), P("seg", "tp"), P("seg", "tp"), P("seg", "tp"), P())
    out_specs = (P(("seg", "tp"), None), P(("seg", "tp"), None), P(("seg", "tp"), None))
    return jax.shard_map(backward, mesh=mesh, in_specs=in_specs, out_specs=out_specs, check_vma=False)
```
